32 devices in a mesh: dp: 8 (over z, x), mp: 4 (over y, core).
Axes of the slice: x: 2, y: 2, z: 4, core: 2. Of those that a mesh axis runs over, the one named last changes fastest.
Arguments:
- teacher_hidden: bfloat16 [4096, 6144], P('dp', 'mp'), may hold values from -4096 to 4096
- teacher_gain: float32 [6144], P('mp'), may hold values from 0.1 to 1.9
- teacher_bias: float32 [6144], P('mp'), may hold values from -3 to 3
- student_feats: bfloat16 [4096, 1024], P(('dp', 'mp')), may hold values from -4096 to 4096
- student_gain: float32 [1024], replicated, may hold values from 0.1 to 1.9
- student_bias: float32 [1024], replicated, may hold values from -3 to 3
- proj_weight: bfloat16 [1024, 6144], P('dp', 'mp'), may hold values from -1.5 to 1.5
Outputs:
- loss: float32 [], replicated
- grad_proj: float32 [1024, 6144], P(None, 'mp')
- grad_feats: bfloat16 [4096, 1024], P(('dp', 'mp'))
- grad_sgain: float32 [1024], replicated
- grad_sbias: float32 [1024], replicated
The draws below stay inside these ranges and needn't reach their ends.
All inputs are finite; a program needn't handle non-finite values.
Results may differ from the reference program's by a relative error of at most 0.014.
Values may be sent and summed in bfloat16 or wider, within the bound.
A program may use at most 64 MiB of HBM per device.

```python
import jax
import jax.numpy as jnp
from jax import lax

DT = 6144
DS = 1024
TOK_DEV = 128
TOKENS = 4096
TBLOCK = 1536
N_DP = 8
N_MP = 4


clip_limit = 4096.0


def latent_rows(key):
    latent_base = jax.random.normal(jax.random.fold_in(key, 101), (TOKENS, DS), jnp.float32)
    spread_part = jax.random.uniform(jax.random.fold_in(key, 102), (TOKENS,), jnp.float32)
    trend_part = jnp.arange(TOKENS, dtype=jnp.float32) / TOKENS
    return (latent_base, 10.0 ** spread_part * 3.0 ** trend_part)


def column_scales(key, width):
    spread_part = jax.random.uniform(key, (width,), jnp.float32)
    trend_part = jnp.arange(width, dtype=jnp.float32) / width
    return 10.0 ** spread_part * 3.0 ** trend_part / 3.0


def draw_student_feats(key, part):
    latent_base, row_scale = latent_rows(key)
    key = jax.random.fold_in(key, 3)
    col_scale = column_scales(jax.random.fold_in(key, 1), DS)
    noise_part = jax.random.normal(jax.random.fold_in(key, 2), (TOKENS, DS), jnp.float32)
    values = (0.8 * latent_base + 0.6 * noise_part) * row_scale[:, None] * col_scale
    return jnp.clip(values, -clip_limit, clip_limit).astype(jnp.bfloat16)


def draw_teacher_hidden(key, part):
    latent_base, row_scale = latent_rows(key)
    key = jax.random.fold_in(key, 5)
    tiled_base = jnp.tile(latent_base, (1, DT // DS))
    col_scale = column_scales(jax.random.fold_in(key, 1), DT)
    position = jnp.arange(TOKENS, dtype=jnp.float32) / TOKENS
    shared_weight = (0.9 - 0.8 * position)[:, None]
    noise_weight = jnp.sqrt(1.0 - shared_weight * shared_weight) + 0.15
    noise_part = jax.random.normal(jax.random.fold_in(key, 2), (TOKENS, DT), jnp.float32)
    values = (shared_weight * tiled_base + noise_weight * noise_part) * row_scale[:, None] * col_scale
    return jnp.clip(values, -clip_limit, clip_limit).astype(jnp.bfloat16)


def draw_proj_weight(key, part):
    key = jax.random.fold_in(key, 7)
    noise_part = jnp.clip(jax.random.normal(key, (DS, DT), jnp.float32), -4.0, 4.0)
    pattern = (jnp.arange(DT)[None, :] % DS == jnp.arange(DS)[:, None]).astype(jnp.float32)
    return (noise_part / jnp.sqrt(DS * 1.0) + 0.8 * pattern).astype(jnp.bfloat16)


def block_levels(rng, extent, split, smallest, largest):
    factor_of = 1.0
    for dim, parts in split:
        heights = jax.random.uniform(jax.random.fold_in(jax.random.fold_in(rng, 6), dim), (parts,), jnp.float32, smallest / len(split), largest / len(split))
        factor_of = factor_of * jnp.repeat(jnp.exp(heights), extent[dim] // parts).reshape((-1,) + (1,) * (len(extent) - 1 - dim))
    return factor_of


def normal_values(rng, shape, spread, reach, split=(), held_as=jnp.bfloat16):
    drawn = jax.random.normal(rng, shape, jnp.float32) * spread
    if len(split) > 0:
        drawn = block_levels(rng, shape, split, -0.22, 0.18) * drawn
    return jnp.clip(drawn, min=-reach, max=reach).astype(held_as)


def setup_inputs(seed: int = 0) -> dict:
    seeds = jax.random.split(jax.random.key(seed), 8)
    teacher_hidden = draw_teacher_hidden(jax.random.fold_in(seeds[7], 71), 0)
    teacher_gain = jnp.clip(1.0 + 0.18 * jax.random.normal(seeds[1], (DT,), jnp.float32), 0.1, 1.9)
    teacher_bias = normal_values(seeds[2], (DT,), 0.5, 3.0, ((0, 4),), jnp.float32)
    student_feats = draw_student_feats(jax.random.fold_in(seeds[7], 71), 0)
    student_gain = jnp.clip(1.0 + 0.18 * jax.random.normal(seeds[4], (DS,), jnp.float32), 0.1, 1.9)
    student_bias = normal_values(seeds[5], (DS,), 0.5, 3.0, (), jnp.float32)
    proj_weight = draw_proj_weight(jax.random.fold_in(seeds[7], 71), 0)
    return {"teacher_hidden": teacher_hidden, "teacher_gain": teacher_gain, "teacher_bias": teacher_bias, "student_feats": student_feats, "student_gain": student_gain, "student_bias": student_bias, "proj_weight": proj_weight}


epsilon = 1e-06
loss_scale = 512.0

def layer_norm(values):
    center = values - lax.optimization_barrier(jnp.mean(values, axis=1, keepdims=True))
    scale = lax.rsqrt(lax.optimization_barrier(jnp.mean(center * center, axis=1, keepdims=True)) + epsilon)
    return (center * scale, scale)

def reference(teacher_hidden, teacher_gain, teacher_bias, student_feats, student_gain, student_bias, proj_weight):
    group_rows = TOK_DEV * N_MP
    hidden_groups = teacher_hidden.reshape(N_DP, group_rows, DT)
    student_groups = student_feats.reshape(N_DP, group_rows, DS)

    def one_group(carry, blocks):
        grad_weight, gain_sum, bias_sum, loss_sum = carry
        hidden_vals, student_rows = blocks
        teacher_hat, unused_scale = layer_norm(hidden_vals.astype(jnp.float32))
        target = teacher_hat * teacher_gain + teacher_bias
        student_hat, student_scale = layer_norm(student_rows.astype(jnp.float32))
        normed = (student_hat * student_gain + student_bias).astype(jnp.bfloat16)
        projected = jnp.dot(normed, proj_weight, preferred_element_type=jnp.float32)
        dot_terms = lax.optimization_barrier(jnp.sum(projected * target, axis=1))
        sq_proj = lax.optimization_barrier(jnp.sum(projected * projected, axis=1))
        sq_target = lax.optimization_barrier(jnp.sum(target * target, axis=1))
        norm_proj = jnp.sqrt(sq_proj + epsilon)
        norm_target = jnp.sqrt(sq_target + epsilon)
        cosine = dot_terms / (norm_proj * norm_target)
        coef_proj = loss_scale * dot_terms / (norm_proj ** 3 * norm_target)
        coef_target = loss_scale / (norm_proj * norm_target)
        grad_out = (coef_proj[:, None] * projected - coef_target[:, None] * target).astype(jnp.bfloat16)
        grad_weight = grad_weight + jnp.dot(normed.T, grad_out, preferred_element_type=jnp.float32)
        block_terms = jnp.einsum('gkw,dkw->kgd', grad_out.reshape(group_rows, N_MP, TBLOCK).astype(jnp.float32), proj_weight.reshape(DS, N_MP, TBLOCK).astype(jnp.float32))
        rounded = lax.optimization_barrier(block_terms.astype(jnp.bfloat16)).astype(jnp.float32)
        grad_normed = lax.optimization_barrier(jnp.sum(rounded, axis=0))
        scaled = grad_normed * student_gain
        grad_rows = (student_scale * (scaled - lax.optimization_barrier(jnp.mean(scaled, axis=1, keepdims=True)) - student_hat * lax.optimization_barrier(jnp.mean(scaled * student_hat, axis=1, keepdims=True)))).astype(jnp.bfloat16)
        new_carry = (grad_weight, gain_sum + lax.optimization_barrier(jnp.sum(grad_normed * student_hat, axis=0)), bias_sum + lax.optimization_barrier(jnp.sum(grad_normed, axis=0)), loss_sum + jnp.sum(1.0 - cosine))
        return (new_carry, grad_rows)
    start_carry = (jnp.zeros((DS, DT), jnp.float32), jnp.zeros((DS,), jnp.float32), jnp.zeros((DS,), jnp.float32), jnp.zeros((), jnp.float32))
    totals, grad_blocks = lax.scan(one_group, start_carry, (hidden_groups, student_groups))
    loss = totals[3] / TOKENS
    return (loss, totals[0], grad_blocks.reshape(TOKENS, DS), totals[1], totals[2])
```

```python
import functools

import jax
import jax.numpy as jnp
from jax import lax
from jax.experimental import pallas as pl
from jax.experimental.pallas import tpu as pltpu
from jax.sharding import PartitionSpec as P

epsilon = 1e-06
loss_scale = 512.0
CHUNK = 64
f32 = jnp.float32
bf16 = jnp.bfloat16


def column_tile(width, most):
    tile = most
    while width % tile:
        tile -= 128
    return tile


def kernel(
    n_dp, n_mp, dt,
    th, tg, tb, sf, sg, sb, w,
    gp_out, gf_out, red_out,
    wfull, gfull, normed, normed_t, own_hat, own_rs, target, proj, go, coef,
    stat_one, stat_two, pb, own_part, rx, zl, zr, zs, gn_send, gn_recv,
    red_mp, red_x, red_z, red_a, red_b, red_c,
    ag_sems, gg_sems, nm_sems, s1_sems, s2_sems, gn_sems, rm_sems, rz_sems, rx_sems, rs_x, rs_r, rs_l, rs_zl, rs_zr,
):
    length = n_dp // 2
    me = lax.axis_index("dp")
    m = lax.axis_index("mp")
    l = me // 2
    p = me % 2
    q = 1 - p
    x_dev = l * 2 + q
    tokens, cols = th.shape
    own, width = sf.shape
    rb = w.shape[0]

    def rows(j, n):
        return pl.ds(pl.multiple_of(j * n, n), n)

    def remote(src, dst, ssem, rsem, device):
        return pltpu.make_async_remote_copy(
            src_ref=src, dst_ref=dst, send_sem=ssem, recv_sem=rsem,
            device_id=device, device_id_type=pl.DeviceIdType.MESH,
        )

    barrier = pltpu.get_barrier_semaphore()
    for k in range(1, n_mp):
        pl.semaphore_signal(barrier, inc=1, device_id={"mp": (m + k) % n_mp}, device_id_type=pl.DeviceIdType.MESH)
    for k in range(1, length):
        pl.semaphore_signal(
            barrier, inc=1, device_id={"dp": ((l + k) % length) * 2 + p}, device_id_type=pl.DeviceIdType.MESH
        )
    pl.semaphore_signal(barrier, inc=1, device_id={"dp": x_dev}, device_id_type=pl.DeviceIdType.MESH)
    pl.semaphore_wait(barrier, n_mp - 1 + length - 1 + 1)

    class Gather:
        def __init__(self, buf, sems):
            self.buf, self.sems = buf, sems

        def block(self, j):
            return self.buf.at[rows(j, rb)]

        def to_right(self, lp):
            ref = self.block(lp * 2 + p)
            return remote(ref, ref, self.sems.at[0, lp], self.sems.at[3, lp], {"dp": lax.rem(me + 2, n_dp)})

        def to_left(self, lp):
            ref = self.block(lp * 2 + p)
            return remote(ref, ref, self.sems.at[1, lp], self.sems.at[3, lp], {"dp": lax.rem(me - 2 + n_dp, n_dp)})

        def to_pair(self, lp):
            ref = self.block(lp * 2 + p)
            return remote(ref, ref, self.sems.at[2, lp], self.sems.at[4, lp], {"dp": x_dev})

        def from_pair(self, lp):
            ref = self.block(lp * 2 + q)
            return remote(ref, ref, self.sems.at[2, lp], self.sems.at[4, lp], {"dp": x_dev})

        def forward_right(self, lp):
            @pl.when(l + 1 < length)
            def _():
                self.to_right(lp).start()

        def forward_left(self, lp):
            @pl.when(l >= 1)
            def _():
                self.to_left(lp).start()

        def begin(self):
            self.forward_right(l)
            self.forward_left(l)
            self.to_pair(l).start()

        def step(self, s):
            a = l - s - 1
            b = l + s + 1

            @pl.when(a >= 0)
            def _():
                self.to_right(a).wait_recv()
                self.forward_right(a)
                self.to_pair(a).start()

            @pl.when(b < length)
            def _():
                self.to_left(b).wait_recv()
                self.forward_left(b)
                self.to_pair(b).start()

        def finish(self):
            for lp in range(length):
                self.from_pair(lp).wait_recv()

        def drain(self):
            for lp in range(length):
                self.to_pair(lp).wait_send()

                @pl.when(jnp.logical_and(lp <= l, l + 1 < length))
                def _():
                    self.to_right(lp).wait_send()

                @pl.when(jnp.logical_and(lp >= l, l >= 1))
                def _():
                    self.to_left(lp).wait_send()

    def mp_peers(make, act):
        for k in range(1, n_mp):
            act(make((m + k) % n_mp))

    def send_all(src, slots, sems):
        mp_peers(lambda d: remote(src(d), slots.at[m], sems.at[0, d], sems.at[1, m], {"mp": d}), lambda c: c.start())

    def recv_all(src, slots, sems):
        mp_peers(lambda d: remote(src(d), slots.at[d], sems.at[0, d], sems.at[1, d], {"mp": d}), lambda c: c.wait_recv())

    def drain_all(src, slots, sems):
        mp_peers(lambda d: remote(src(d), slots.at[m], sems.at[0, d], sems.at[1, m], {"mp": d}), lambda c: c.wait_send())

    gather_w = Gather(wfull, ag_sems)
    wfull[rows(me, rb)] = w[...]
    gather_w.begin()

    for c in range(own // CHUNK):
        r = pl.ds(c * CHUNK, CHUNK)
        v = sf[r].astype(f32)
        v = v - jnp.mean(v, axis=1, keepdims=True)
        rs = lax.rsqrt(jnp.mean(v * v, axis=1, keepdims=True) + epsilon)
        hat = v * rs
        own_hat[r] = hat
        own_rs[r] = jnp.broadcast_to(rs, (CHUNK, 128))
        normed[m, r] = (hat * sg[...] + sb[...]).astype(bf16)
    nm_src = lambda d: normed.at[m]
    send_all(nm_src, normed, nm_sems)

    lane = lax.broadcasted_iota(jnp.int32, (CHUNK, 128), 1)

    @pl.loop(0, tokens // CHUNK)
    def _(c):
        r = rows(c, CHUNK)
        v = th[r].astype(f32)
        mean = jnp.sum(v, axis=1, keepdims=True) / cols
        v = v - mean
        sq = jnp.sum(v * v, axis=1, keepdims=True)
        coef[r] = jnp.where(lane == 0, mean, jnp.where(lane == 1, sq, 0.0))

    stat_one[m] = coef[...].T[0:8]
    s1_src = lambda d: stat_one.at[m]
    send_all(s1_src, stat_one, s1_sems)
    recv_all(s1_src, stat_one, s1_sems)
    mean = stat_one[0, 0:1]
    for k in range(1, n_mp):
        mean = mean + stat_one[k, 0:1]
    mean = mean / n_mp
    total = jnp.zeros_like(mean)
    for k in range(n_mp):
        gap = stat_one[k, 0:1] - mean
        total = total + (stat_one[k, 1:2] + cols * (gap * gap))
    scale = lax.rsqrt(total / dt + epsilon)
    coef[...] = jnp.concatenate([mean, scale, jnp.zeros((126, tokens), f32)], axis=0).T

    @pl.loop(0, tokens // CHUNK)
    def _(c):
        r = rows(c, CHUNK)
        cf = coef[r]
        t = (th[r].astype(f32) - cf[:, 0:1]) * cf[:, 1:2] * tg[...] + tb[...]
        target[r] = t
        coef[r] = jnp.broadcast_to(jnp.sum(t * t, axis=1, keepdims=True), (CHUNK, 128))

    gather_w.step(0)
    recv_all(nm_src, normed, nm_sems)
    for k in range(n_mp):
        normed_t[:, pl.ds(k * own, own)] = normed[k].T
    for s in range(1, length - 1):
        gather_w.step(s)
    gather_w.finish()

    tile = column_tile(cols, 256)

    @pl.loop(0, cols // tile)
    def _(c):
        ct = rows(c, tile)
        proj[:, ct] = jnp.dot(
            normed[...].reshape(tokens, width), wfull[:, ct], preferred_element_type=f32
        )

    @pl.loop(0, tokens // CHUNK)
    def _(c):
        r = rows(c, CHUNK)
        pv, t = proj[r], target[r]
        inner = jnp.sum(pv * t, axis=1, keepdims=True)
        sq = jnp.sum(pv * pv, axis=1, keepdims=True)
        coef[r] = jnp.where(lane == 0, inner, jnp.where(lane == 1, sq, coef[r]))

    stat_two[m] = coef[...].T[0:8]
    s2_src = lambda d: stat_two.at[m]
    send_all(s2_src, stat_two, s2_sems)
    recv_all(s2_src, stat_two, s2_sems)
    sums = stat_two[0]
    for k in range(1, n_mp):
        sums = sums + stat_two[k]
    inner = sums[0:1]
    norm_proj = jnp.sqrt(sums[1:2] + epsilon)
    norm_target = jnp.sqrt(sums[2:3] + epsilon)
    both = norm_proj * norm_target
    loss_part = jnp.sum(1.0 - inner / both, axis=1, keepdims=True)
    coef_proj = loss_scale * inner / (norm_proj * norm_proj * norm_proj * norm_target)
    coef_target = loss_scale / both
    coef[...] = jnp.concatenate([coef_proj, coef_target, jnp.zeros((126, tokens), f32)], axis=0).T

    @pl.loop(0, tokens // CHUNK)
    def _(c):
        r = rows(c, CHUNK)
        cf = coef[r]
        go[r] = (cf[:, 0:1] * proj[r] - cf[:, 1:2] * target[r]).astype(bf16)

    near = jnp.minimum(l, length - 1 - l)
    alone = length - 1 - 2 * near

    def order(i):
        far = jnp.where(2 * l < length, length - 1 - i, i)
        k = jnp.maximum(i - alone, 0)
        d = near - k // 2
        return jnp.where(i < alone, far, jnp.where(k % 2 == 0, l + d, l - d))

    wide = column_tile(cols, 512)

    def partial(j, c):
        return jnp.dot(normed_t[rows(j, rb)], go[:, pl.ds(c * wide, wide)], preferred_element_type=f32)

    def x_copy(lp):
        return remote(pb.at[lp], rx.at[lp], rs_x.at[0, lp], rs_x.at[1, lp], {"dp": x_dev})

    @pl.loop(0, length)
    def _(i):
        lp = order(i)
        for c in range(cols // wide):
            pb[lp, :, pl.ds(c * wide, wide)] = partial(lp * 2 + q, c).astype(bf16)
        x_copy(lp).start()

    @pl.loop(0, length)
    def _(i):
        lp = order(i)
        for c in range(cols // wide):
            own_part[lp, :, pl.ds(c * wide, wide)] = partial(lp * 2 + p, c)

    band = 256

    @pl.loop(0, width // band)
    def _(c):
        ct = rows(c, band)
        g = lax.dot_general(go[...], wfull[ct], (((1,), (1,)), ((), ())), preferred_element_type=f32)
        for k in range(n_mp):
            gn_send[k, :, ct] = g[k * own:(k + 1) * own].astype(bf16)

    gn_src = lambda d: gn_send.at[d]
    send_all(gn_src, gn_recv, gn_sems)
    gn_recv[m] = gn_send[m]

    gather_g = Gather(gfull, gg_sems)

    def right_copy(lp):
        return remote(zs.at[lp], zl.at[lp], rs_r.at[lp], rs_zl.at[lp], {"dp": lax.rem(me + 2, n_dp)})

    def left_copy(lp):
        return remote(zs.at[lp], zr.at[lp], rs_l.at[lp], rs_zr.at[lp], {"dp": lax.rem(me - 2 + n_dp, n_dp)})

    @pl.loop(0, length)
    def _(i):
        lp = order(i)
        x_copy(lp).wait_recv()

        @pl.when(jnp.logical_and(lp >= l, l > 0))
        def _():
            right_copy(lp).wait_recv()
            own_part[lp] = own_part[lp] + zl[lp].astype(f32)

        @pl.when(jnp.logical_and(lp <= l, l < length - 1))
        def _():
            left_copy(lp).wait_recv()
            own_part[lp] = own_part[lp] + zr[lp].astype(f32)

        zs[lp] = (own_part[lp] + rx[lp].astype(f32)).astype(bf16)

        @pl.when(lp > l)
        def _():
            right_copy(lp).start()

        @pl.when(lp < l)
        def _():
            left_copy(lp).start()

    gfull[rows(me, rb)] = zs[l]
    gather_g.begin()

    recv_all(gn_src, gn_recv, gn_sems)
    gain_sum = jnp.zeros((1, width), f32)
    bias_sum = jnp.zeros((1, width), f32)
    for c in range(own // CHUNK):
        r = pl.ds(c * CHUNK, CHUNK)
        g = gn_recv[0, r].astype(f32)
        for k in range(1, n_mp):
            g = g + gn_recv[k, r].astype(f32)
        hat = own_hat[r]
        gain_sum = gain_sum + jnp.sum(g * hat, axis=0, keepdims=True)
        bias_sum = bias_sum + jnp.sum(g, axis=0, keepdims=True)
        g = g * sg[...]
        g = g - jnp.mean(g, axis=1, keepdims=True) - hat * jnp.mean(g * hat, axis=1, keepdims=True)
        gf_out[r] = (own_rs[r][:, 0:1] * g).astype(bf16)
    red_mp[m] = jnp.concatenate(
        [gain_sum, bias_sum, jnp.broadcast_to(loss_part, (1, width)), jnp.zeros((5, width), f32)], axis=0
    )
    rm_src = lambda d: red_mp.at[m]
    send_all(rm_src, red_mp, rm_sems)
    gather_g.step(0)
    recv_all(rm_src, red_mp, rm_sems)
    acc = red_mp[0]
    for k in range(1, n_mp):
        acc = acc + red_mp[k]
    red_a[...] = acc
    pair = remote(red_a, red_x, rx_sems.at[0], rx_sems.at[1], {"dp": x_dev})
    pair.start()
    if length > 2:
        gather_g.step(1)
    pair.wait_recv()
    red_z[l] = red_a[...] + red_x[...]

    def line_copy(d, slot):
        return remote(red_z.at[l], red_z.at[slot], rz_sems.at[0, d], rz_sems.at[1, slot], {"dp": d * 2 + p})

    for k in range(1, length):
        line_copy((l + k) % length, l).start()
    for s in range(2, length - 1):
        gather_g.step(s)
    for k in range(1, length):
        line_copy((l + k) % length, (l + k) % length).wait_recv()
    acc = red_z[0]
    for k in range(1, length):
        acc = acc + red_z[k]
    red_out[...] = acc

    gather_g.finish()
    gp_out[...] = gfull[...]

    gather_w.drain()
    gather_g.drain()
    drain_all(nm_src, normed, nm_sems)
    drain_all(s1_src, stat_one, s1_sems)
    drain_all(s2_src, stat_two, s2_sems)
    drain_all(gn_src, gn_recv, gn_sems)
    drain_all(rm_src, red_mp, rm_sems)
    pair.wait_send()
    for k in range(1, length):
        line_copy((l + k) % length, l).wait_send()
    for lp in range(length):
        x_copy(lp).wait_send()

        @pl.when(lp > l)
        def _():
            right_copy(lp).wait_send()

        @pl.when(lp < l)
        def _():
            left_copy(lp).wait_send()


def per_device(n_dp, n_mp, dt, th, tg, tb, sf, sg, sb, w):
    tokens, cols = th.shape
    own, width = sf.shape
    rb = w.shape[0]
    length = n_dp // 2
    vmem = pltpu.VMEM
    dma = pltpu.SemaphoreType.DMA
    scratch = [
        vmem((width, cols), bf16),
        vmem((width, cols), bf16),
        vmem((n_mp, own, width), bf16),
        vmem((width, tokens), bf16),
        vmem((own, width), f32),
        vmem((own, 128), f32),
        vmem((tokens, cols), f32),
        vmem((tokens, cols), f32),
        vmem((tokens, cols), bf16),
        vmem((tokens, 128), f32),
        vmem((n_mp, 8, tokens), f32),
        vmem((n_mp, 8, tokens), f32),
        vmem((length, rb, cols), bf16),
        vmem((length, rb, cols), f32),
        vmem((length, rb, cols), bf16),
        vmem((length, rb, cols), bf16),
        vmem((length, rb, cols), bf16),
        vmem((length, rb, cols), bf16),
        vmem((n_mp, own, width), bf16),
        vmem((n_mp, own, width), bf16),
        vmem((n_mp, 8, width), f32),
        vmem((8, width), f32),
        vmem((length, 8, width), f32),
        vmem((8, width), f32),
        vmem((8, width), f32),
        vmem((8, width), f32),
        dma((5, length)), dma((5, length)),
        dma((2, n_mp)), dma((2, n_mp)), dma((2, n_mp)), dma((2, n_mp)), dma((2, n_mp)),
        dma((2, length)), dma((2,)), dma((2, length)),
        dma((length,)), dma((length,)), dma((length,)), dma((length,)),
    ]
    whole = pl.BlockSpec(memory_space=pltpu.VMEM)
    grad_proj, grad_feats, sums = pl.pallas_call(
        functools.partial(kernel, n_dp, n_mp, dt),
        out_shape=(
            jax.ShapeDtypeStruct((width, cols), bf16),
            jax.ShapeDtypeStruct((own, width), bf16),
            jax.ShapeDtypeStruct((8, width), f32),
        ),
        in_specs=[whole] * 7,
        out_specs=(whole, whole, whole),
        scratch_shapes=scratch,
        compiler_params=pltpu.CompilerParams(
            collective_id=0, has_side_effects=True, vmem_limit_bytes=56 * 1024 * 1024
        ),
    )(th, tg.reshape(1, -1), tb.reshape(1, -1), sf, sg.reshape(1, -1), sb.reshape(1, -1), w)
    loss = sums[2, 0] / (n_mp * tokens * n_dp)
    return (loss, grad_proj.astype(f32), grad_feats, sums[0], sums[1])


def solution(mesh):
    n_dp, n_mp = mesh.shape["dp"], mesh.shape["mp"]

    def run(th, tg, tb, sf, sg, sb, w):
        in_specs = (P("dp", "mp"), P("mp"), P("mp"), P(("dp", "mp"), None), P(), P(), P("dp", "mp"))
        out_specs = (P(), P(None, "mp"), P(("dp", "mp"), None), P(), P())
        return jax.shard_map(
            functools.partial(per_device, n_dp, n_mp, th.shape[1]),
            mesh=mesh, in_specs=in_specs, out_specs=out_specs, check_vma=False,
        )(th, tg, tb, sf, sg, sb, w)

    return run
```

```python
import functools

import jax
import jax.numpy as jnp
from jax import lax
from jax.experimental import pallas as pl
from jax.experimental.pallas import tpu as pltpu
from jax.sharding import PartitionSpec as P

epsilon = 1e-06
loss_scale = 512.0
CHUNK = 64
f32 = jnp.float32
bf16 = jnp.bfloat16


def column_tile(width, most):
    tile = most
    while width % tile:
        tile -= 128
    return tile


def split_columns(cols):
    unit = 256 if cols % 256 == 0 and cols >= 1024 else 128
    n = cols // unit
    last = max(1, (n + 3) // 6)
    first = (n - last + 1) // 2
    cuts = [0, first * unit, (n - last) * unit, cols]
    return list(zip(cuts[:-1], cuts[1:]))


def kernel(
    n_dp, n_mp, dt,
    th, tg_ref, tb_ref, sf, sg_ref, sb_ref, w,
    gp_out, gf_out, gain_out, bias_out, loss_out,
    wfull, gfull, normed, normed_t, own_hat, own_rs, target, proj, go, coef,
    stat_one, stat_two, pb, own_part, rx, zl, zr, zs, b_part, b_zl, b_zr, b_zs, b_x, gn_send, gn_recv,
    red_mp, red_x, red_z, red_a,
    ag_sems, gg_sems, nm_sems, s1_sems, s2_sems, gn_sems, rm_sems, rz_sems, rx_sems, rs_sems, rb_sems, bx_sems,
):
    length = n_dp // 2
    me = lax.axis_index("dp")
    m = lax.axis_index("mp")
    l = me // 2
    p = me % 2
    q = 1 - p
    x_dev = l * 2 + q
    right_dev = lax.rem(me + 2, n_dp)
    left_dev = lax.rem(me - 2 + n_dp, n_dp)
    tokens, cols = th.shape
    own, width = sf.shape
    rb = w.shape[0]
    chunks = split_columns(cols)
    tg, tb = tg_ref[...].reshape(1, cols), tb_ref[...].reshape(1, cols)
    sg, sb = sg_ref[...].reshape(1, width), sb_ref[...].reshape(1, width)

    def rows(j, n):
        return pl.ds(pl.multiple_of(j * n, n), n)

    def span(chunk):
        return pl.ds(chunk[0], chunk[1] - chunk[0])

    def remote(src, dst, ssem, rsem, device):
        return pltpu.make_async_remote_copy(
            src_ref=src, dst_ref=dst, send_sem=ssem, recv_sem=rsem,
            device_id=device, device_id_type=pl.DeviceIdType.MESH,
        )

    barrier = pltpu.get_barrier_semaphore()
    for k in range(1, n_mp):
        pl.semaphore_signal(barrier, inc=1, device_id={"mp": (m + k) % n_mp}, device_id_type=pl.DeviceIdType.MESH)
    for k in range(1, length):
        pl.semaphore_signal(
            barrier, inc=1, device_id={"dp": ((l + k) % length) * 2 + p}, device_id_type=pl.DeviceIdType.MESH
        )
    pl.semaphore_signal(barrier, inc=1, device_id={"dp": x_dev}, device_id_type=pl.DeviceIdType.MESH)
    pl.semaphore_wait(barrier, n_mp - 1 + length - 1 + 1)

    class Gather:
        def __init__(self, buf, sems, chunk, line_first):
            self.buf, self.sems, self.chunk, self.line_first = buf, sems, chunk, line_first
            self.lines = ((0, p),) if line_first else ((0, p), (1, q))

        def copy(self, lp, pp, ssem, rsem, device):
            ref = self.buf.at[rows(lp * 2 + pp, rb), span(self.chunk)]
            return remote(ref, ref, self.sems.at[ssem, lp], self.sems.at[rsem, lp], {"dp": device})

        def right(self, lp, pp, k):
            return self.copy(lp, pp, k, 2 + k, right_dev)

        def left(self, lp, pp, k):
            return self.copy(lp, pp, 4 + k, 2 + k, left_dev)

        def pair(self, lp, pp):
            return self.copy(lp, pp, 6, 7, x_dev)

        def forward_right(self, lp, pp, k):
            @pl.when(l + 1 < length)
            def _():
                self.right(lp, pp, k).start()

        def forward_left(self, lp, pp, k):
            @pl.when(l >= 1)
            def _():
                self.left(lp, pp, k).start()

        def begin(self):
            self.pair(l, p).start()
            self.forward_right(l, p, 0)
            self.forward_left(l, p, 0)

        def middle(self):
            self.pair(l, q).wait_recv()
            self.forward_right(l, q, 1)
            self.forward_left(l, q, 1)

        def step(self, s):
            a = l - s - 1
            b = l + s + 1
            for k, pp in self.lines:
                @pl.when(a >= 0)
                def _():
                    self.right(a, pp, k).wait_recv()
                    self.forward_right(a, pp, k)
                    if self.line_first:
                        self.pair(a, pp).start()

                @pl.when(b < length)
                def _():
                    self.left(b, pp, k).wait_recv()
                    self.forward_left(b, pp, k)
                    if self.line_first:
                        self.pair(b, pp).start()

        def finish(self):
            if self.line_first:
                @pl.loop(0, length)
                def _(lp):
                    self.pair(lp, q).wait_recv()

        def drain(self):
            @pl.loop(0, length)
            def _(lp):
                if self.line_first:
                    self.pair(lp, p).wait_send()
                for k, pp in self.lines:
                    @pl.when(jnp.logical_and(lp <= l, l + 1 < length))
                    def _():
                        self.right(lp, pp, k).wait_send()

                    @pl.when(jnp.logical_and(lp >= l, l >= 1))
                    def _():
                        self.left(lp, pp, k).wait_send()
            if not self.line_first:
                self.pair(l, p).wait_send()

    def gathers(buf, sems):
        return [Gather(buf, sems.at[i], chunks[i], i < 2) for i in range(3)]

    def mp_peers(make, act):
        for k in range(1, n_mp):
            act(make((m + k) % n_mp))

    def send_all(src, slots, sems):
        mp_peers(lambda d: remote(src(d), slots.at[m], sems.at[0, d], sems.at[1, m], {"mp": d}), lambda c: c.start())

    def recv_all(src, slots, sems):
        mp_peers(lambda d: remote(src(d), slots.at[d], sems.at[0, d], sems.at[1, d], {"mp": d}), lambda c: c.wait_recv())

    def drain_all(src, slots, sems):
        mp_peers(lambda d: remote(src(d), slots.at[m], sems.at[0, d], sems.at[1, m], {"mp": d}), lambda c: c.wait_send())

    gather_w = gathers(wfull, ag_sems)
    wfull[rows(me, rb)] = w[...]
    for g in (gather_w[2], gather_w[0], gather_w[1]):
        g.begin()

    for c in range(own // CHUNK):
        r = pl.ds(c * CHUNK, CHUNK)
        v = sf[r].astype(f32)
        v = v - jnp.mean(v, axis=1, keepdims=True)
        rs = lax.rsqrt(jnp.mean(v * v, axis=1, keepdims=True) + epsilon)
        hat = v * rs
        own_hat[r] = hat
        own_rs[r] = jnp.broadcast_to(rs, (CHUNK, 128))
        normed[m, r] = (hat * sg + sb).astype(bf16)
    nm_src = lambda d: normed.at[m]
    send_all(nm_src, normed, nm_sems)

    lane = lax.broadcasted_iota(jnp.int32, (CHUNK, 128), 1)

    @pl.loop(0, tokens // CHUNK)
    def _(c):
        r = rows(c, CHUNK)
        v = th[r].astype(f32)
        mean = jnp.sum(v, axis=1, keepdims=True) / cols
        v = v - mean
        sq = jnp.sum(v * v, axis=1, keepdims=True)
        coef[r] = jnp.where(lane == 0, mean, jnp.where(lane == 1, sq, 0.0))

    stat_one[m] = coef[...].T[0:8]
    s1_src = lambda d: stat_one.at[m]
    send_all(s1_src, stat_one, s1_sems)
    recv_all(s1_src, stat_one, s1_sems)
    mean = stat_one[0, 0:1]
    for k in range(1, n_mp):
        mean = mean + stat_one[k, 0:1]
    mean = mean / n_mp
    total = jnp.zeros_like(mean)
    for k in range(n_mp):
        gap = stat_one[k, 0:1] - mean
        total = total + (stat_one[k, 1:2] + cols * (gap * gap))
    scale = lax.rsqrt(total / dt + epsilon)
    coef[...] = jnp.concatenate([mean, scale, jnp.zeros((126, tokens), f32)], axis=0).T

    @pl.loop(0, tokens // CHUNK)
    def _(c):
        r = rows(c, CHUNK)
        cf = coef[r]
        t = (th[r].astype(f32) - cf[:, 0:1]) * cf[:, 1:2] * tg + tb
        target[r] = t
        coef[r] = jnp.where(lane == 2, jnp.sum(t * t, axis=1, keepdims=True), 0.0)

    gather_w[2].middle()
    for g in gather_w:
        g.step(0)
    recv_all(nm_src, normed, nm_sems)
    for k in range(n_mp):
        normed_t[:, pl.ds(k * own, own)] = normed[k].T

    @pl.loop(1, length - 1)
    def _(s):
        for g in gather_w:
            g.step(s)

    for g, (c0, c1) in zip(gather_w, chunks):
        g.finish()
        tile = column_tile(c1 - c0, 256)

        @pl.loop(0, (c1 - c0) // tile)
        def _(c):
            ct = pl.ds(pl.multiple_of(c0 + c * tile, 128), tile)
            proj[:, ct] = jnp.dot(
                normed[...].reshape(tokens, width), wfull[:, ct], preferred_element_type=f32
            )

        @pl.loop(0, tokens // CHUNK)
        def _(c):
            r = rows(c, CHUNK)
            pv, t = proj[r, c0:c1], target[r, c0:c1]
            inner = jnp.sum(pv * t, axis=1, keepdims=True)
            sq = jnp.sum(pv * pv, axis=1, keepdims=True)
            coef[r] = coef[r] + jnp.where(lane == 0, inner, jnp.where(lane == 1, sq, 0.0))

    stat_two[m] = coef[...].T[0:8]
    s2_src = lambda d: stat_two.at[m]
    send_all(s2_src, stat_two, s2_sems)
    recv_all(s2_src, stat_two, s2_sems)
    sums = stat_two[0]
    for k in range(1, n_mp):
        sums = sums + stat_two[k]
    inner = sums[0:1]
    norm_proj = jnp.sqrt(sums[1:2] + epsilon)
    norm_target = jnp.sqrt(sums[2:3] + epsilon)
    both = norm_proj * norm_target
    loss_part = jnp.sum(1.0 - inner / both, axis=1, keepdims=True)
    coef_proj = loss_scale * inner / (norm_proj * norm_proj * norm_proj * norm_target)
    coef_target = loss_scale / both
    coef[...] = jnp.concatenate([coef_proj, coef_target, jnp.zeros((126, tokens), f32)], axis=0).T

    def make_go(chunk):
        @pl.loop(0, tokens // CHUNK)
        def _(c):
            r = rows(c, CHUNK)
            cf = coef[r]
            ct = span(chunk)
            go[r, ct] = (cf[:, 0:1] * proj[r, ct] - cf[:, 1:2] * target[r, ct]).astype(bf16)

    near = jnp.minimum(l, length - 1 - l)
    alone = length - 1 - 2 * near

    def order(i):
        far = jnp.where(2 * l < length, length - 1 - i, i)
        k = jnp.maximum(i - alone, 0)
        d = near - k // 2
        return jnp.where(i < alone, far, jnp.where(k % 2 == 0, l + d, l - d))

    def partial(j, chunk):
        return jnp.dot(normed_t[rows(j, rb)], go[:, span(chunk)], preferred_element_type=f32)

    def x_copy(i, lp):
        part = span(chunks[i])
        return remote(pb.at[lp, :, part], rx.at[lp, :, part], rs_sems.at[i, 0, lp], rs_sems.at[i, 1, lp], {"dp": x_dev})

    def right_copy(i, lp):
        part = span(chunks[i])
        return remote(
            zs.at[lp, :, part], zl.at[lp, :, part], rs_sems.at[i, 2, lp], rs_sems.at[i, 3, lp], {"dp": right_dev}
        )

    def left_copy(i, lp):
        part = span(chunks[i])
        return remote(
            zs.at[lp, :, part], zr.at[lp, :, part], rs_sems.at[i, 4, lp], rs_sems.at[i, 5, lp], {"dp": left_dev}
        )

    def b_right(lp):
        return remote(b_zs.at[lp], b_zl.at[lp], rb_sems.at[0, lp], rb_sems.at[1, lp], {"dp": right_dev})

    def b_left(lp):
        return remote(b_zs.at[lp], b_zr.at[lp], rb_sems.at[2, lp], rb_sems.at[3, lp], {"dp": left_dev})

    def b_pair():
        return remote(b_zs.at[l, q], b_x, bx_sems.at[0], bx_sems.at[1], {"dp": x_dev})

    def scatter(i, lp):
        part = span(chunks[i])
        x_copy(i, lp).wait_recv()

        @pl.when(jnp.logical_and(lp >= l, l > 0))
        def _():
            right_copy(i, lp).wait_recv()
            own_part[lp, :, part] = own_part[lp, :, part] + zl[lp, :, part].astype(f32)

        @pl.when(jnp.logical_and(lp <= l, l < length - 1))
        def _():
            left_copy(i, lp).wait_recv()
            own_part[lp, :, part] = own_part[lp, :, part] + zr[lp, :, part].astype(f32)

        zs[lp, :, part] = (own_part[lp, :, part] + rx[lp, :, part].astype(f32)).astype(bf16)

        @pl.when(lp > l)
        def _():
            right_copy(i, lp).start()

        @pl.when(lp < l)
        def _():
            left_copy(i, lp).start()

    def b_scatter(lp):
        @pl.when(jnp.logical_and(lp >= l, l > 0))
        def _():
            b_right(lp).wait_recv()
            b_part[lp] = b_part[lp] + b_zl[lp].astype(f32)

        @pl.when(jnp.logical_and(lp <= l, l < length - 1))
        def _():
            b_left(lp).wait_recv()
            b_part[lp] = b_part[lp] + b_zr[lp].astype(f32)

        b_zs[lp] = b_part[lp].astype(bf16)

        @pl.when(lp > l)
        def _():
            b_right(lp).start()

        @pl.when(lp < l)
        def _():
            b_left(lp).start()

        @pl.when(lp == l)
        def _():
            b_pair().start()

    last = chunks[2]
    make_go(last)
    b_part[...] = jnp.dot(normed_t[...], go[:, span(last)], preferred_element_type=f32).reshape(b_part.shape)

    at_end = jnp.logical_or(l == 0, l == length - 1)

    @pl.when(at_end)
    def _():
        @pl.loop(0, length - 1)
        def _(n):
            b_scatter(order(n))

    for i in range(2):
        make_go(chunks[i])

        @pl.loop(0, length)
        def _(n):
            lp = order(n)
            pb[lp, :, span(chunks[i])] = partial(lp * 2 + q, chunks[i]).astype(bf16)
            x_copy(i, lp).start()

    for i in range(2):
        @pl.loop(0, length)
        def _(n):
            lp = order(n)
            own_part[lp, :, span(chunks[i])] = partial(lp * 2 + p, chunks[i])

    band = 256

    @pl.loop(0, width // band)
    def _(c):
        ct = rows(c, band)
        g = lax.dot_general(go[...], wfull[ct], (((1,), (1,)), ((), ())), preferred_element_type=f32)
        for k in range(n_mp):
            gn_send[k, :, ct] = g[k * own:(k + 1) * own].astype(bf16)

    gn_src = lambda d: gn_send.at[d]
    send_all(gn_src, gn_recv, gn_sems)
    gn_recv[m] = gn_send[m]

    gather_g = gathers(gfull, gg_sems)

    @pl.loop(0, length)
    def _(n):
        lp = order(n)

        @pl.when(jnp.logical_or(jnp.logical_not(at_end), n == length - 1))
        def _():
            b_scatter(lp)

        scatter(0, lp)

    gfull[rows(me, rb), span(chunks[0])] = zs[l, :, span(chunks[0])]
    gather_g[0].begin()

    scatter(1, order(0))
    b_pair().wait_recv()
    gfull[rows(me, rb), span(last)] = (b_part[l, p] + b_x[...].astype(f32)).astype(bf16)
    gather_g[2].begin()

    recv_all(gn_src, gn_recv, gn_sems)
    gain_sum = jnp.zeros((1, width), f32)
    bias_sum = jnp.zeros((1, width), f32)
    for c in range(own // CHUNK):
        r = pl.ds(c * CHUNK, CHUNK)
        g = gn_recv[0, r].astype(f32)
        for k in range(1, n_mp):
            g = g + gn_recv[k, r].astype(f32)
        hat = own_hat[r]
        gain_sum = gain_sum + jnp.sum(g * hat, axis=0, keepdims=True)
        bias_sum = bias_sum + jnp.sum(g, axis=0, keepdims=True)
        g = g * sg
        g = g - jnp.mean(g, axis=1, keepdims=True) - hat * jnp.mean(g * hat, axis=1, keepdims=True)
        gf_out[r] = (own_rs[r][:, 0:1] * g).astype(bf16)
    red_mp[m] = jnp.concatenate(
        [gain_sum, bias_sum, jnp.broadcast_to(loss_part, (1, width)), jnp.zeros((5, width), f32)], axis=0
    )
    rm_src = lambda d: red_mp.at[m]
    send_all(rm_src, red_mp, rm_sems)
    gather_g[0].step(0)
    gather_g[2].middle()

    @pl.loop(1, length - 1)
    def _(n):
        scatter(1, order(n))
        gather_g[0].step(n)
        gather_g[2].step(n - 1)

    scatter(1, order(length - 1))
    gfull[rows(me, rb), span(chunks[1])] = zs[l, :, span(chunks[1])]
    gather_g[1].begin()
    gather_g[2].step(length - 2)

    recv_all(rm_src, red_mp, rm_sems)
    acc = red_mp[0]
    for k in range(1, n_mp):
        acc = acc + red_mp[k]
    red_a[...] = acc
    pair = remote(red_a, red_x, rx_sems.at[0], rx_sems.at[1], {"dp": x_dev})
    pair.start()
    gather_g[1].step(0)
    pair.wait_recv()
    red_z[l] = red_a[...] + red_x[...]

    def line_copy(d, slot):
        return remote(red_z.at[l], red_z.at[slot], rz_sems.at[0, d], rz_sems.at[1, slot], {"dp": d * 2 + p})

    for k in range(1, length):
        line_copy((l + k) % length, l).start()

    @pl.loop(1, length - 1)
    def _(s):
        gather_g[1].step(s)

    for k in range(1, length):
        line_copy((l + k) % length, (l + k) % length).wait_recv()
    acc = red_z[0]
    for k in range(1, length):
        acc = acc + red_z[k]
    gain_out[...] = acc[0:1].reshape(width)
    bias_out[...] = acc[1:2].reshape(width)
    loss_out[...] = acc[2:3, 0:128] / (n_mp * tokens * n_dp)

    gather_g[0].finish()
    gather_g[2].finish()
    gather_g[1].finish()
    gp_out[...] = gfull[...]

    for g in gather_w + gather_g:
        g.drain()
    drain_all(nm_src, normed, nm_sems)
    drain_all(s1_src, stat_one, s1_sems)
    drain_all(s2_src, stat_two, s2_sems)
    drain_all(gn_src, gn_recv, gn_sems)
    drain_all(rm_src, red_mp, rm_sems)
    pair.wait_send()
    for k in range(1, length):
        line_copy((l + k) % length, l).wait_send()
    b_pair().wait_send()

    @pl.loop(0, length)
    def _(lp):
        for i in range(2):
            x_copy(i, lp).wait_send()

        @pl.when(lp > l)
        def _():
            for i in range(2):
                right_copy(i, lp).wait_send()
            b_right(lp).wait_send()

        @pl.when(lp < l)
        def _():
            for i in range(2):
                left_copy(i, lp).wait_send()
            b_left(lp).wait_send()


def per_device(n_dp, n_mp, dt, th, tg, tb, sf, sg, sb, w):
    tokens, cols = th.shape
    own, width = sf.shape
    rb = w.shape[0]
    length = n_dp // 2
    chunks = split_columns(cols)
    bw = chunks[2][1] - chunks[2][0]
    vmem = pltpu.VMEM
    dma = pltpu.SemaphoreType.DMA
    scratch = [
        vmem((width, cols), bf16),
        vmem((width, cols), bf16),
        vmem((n_mp, own, width), bf16),
        vmem((width, tokens), bf16),
        vmem((own, width), f32),
        vmem((own, 128), f32),
        vmem((tokens, cols), f32),
        vmem((tokens, cols), f32),
        vmem((tokens, cols), bf16),
        vmem((tokens, 128), f32),
        vmem((n_mp, 8, tokens), f32),
        vmem((n_mp, 8, tokens), f32),
        vmem((length, rb, cols), bf16),
        vmem((length, rb, cols), f32),
        vmem((length, rb, cols), bf16),
        vmem((length, rb, cols), bf16),
        vmem((length, rb, cols), bf16),
        vmem((length, rb, cols), bf16),
        vmem((length, 2, rb, bw), f32),
        vmem((length, 2, rb, bw), bf16),
        vmem((length, 2, rb, bw), bf16),
        vmem((length, 2, rb, bw), bf16),
        vmem((rb, bw), bf16),
        vmem((n_mp, own, width), bf16),
        vmem((n_mp, own, width), bf16),
        vmem((n_mp, 8, width), f32),
        vmem((8, width), f32),
        vmem((length, 8, width), f32),
        vmem((8, width), f32),
        dma((3, 8, length)), dma((3, 8, length)),
        dma((2, n_mp)), dma((2, n_mp)), dma((2, n_mp)), dma((2, n_mp)), dma((2, n_mp)),
        dma((2, length)), dma((2,)), dma((2, 6, length)), dma((4, length)), dma((2,)),
    ]
    whole = pl.BlockSpec(memory_space=pltpu.VMEM)
    grad_proj, grad_feats, gain, bias, loss = pl.pallas_call(
        functools.partial(kernel, n_dp, n_mp, dt),
        out_shape=(
            jax.ShapeDtypeStruct((width, cols), bf16),
            jax.ShapeDtypeStruct((own, width), bf16),
            jax.ShapeDtypeStruct((width,), f32),
            jax.ShapeDtypeStruct((width,), f32),
            jax.ShapeDtypeStruct((1, 128), f32),
        ),
        in_specs=[whole] * 7,
        out_specs=(whole,) * 5,
        scratch_shapes=scratch,
        compiler_params=pltpu.CompilerParams(
            collective_id=0, has_side_effects=True, vmem_limit_bytes=56 * 1024 * 1024
        ),
    )(th, tg, tb, sf, sg, sb, w)
    return (loss[0, 0], grad_proj.astype(f32), grad_feats, gain, bias)


def solution(mesh):
    n_dp, n_mp = mesh.shape["dp"], mesh.shape["mp"]

    def run(th, tg, tb, sf, sg, sb, w):
        in_specs = (P("dp", "mp"), P("mp"), P("mp"), P(("dp", "mp"), None), P(), P(), P("dp", "mp"))
        out_specs = (P(), P(None, "mp"), P(("dp", "mp"), None), P(), P())
        return jax.shard_map(
            functools.partial(per_device, n_dp, n_mp, th.shape[1]),
            mesh=mesh, in_specs=in_specs, out_specs=out_specs, check_vma=False,
        )(th, tg, tb, sf, sg, sb, w)

    return run
```

```python
import functools

import jax
import jax.numpy as jnp
from jax import lax
from jax.experimental import pallas as pl
from jax.experimental.pallas import tpu as pltpu
from jax.sharding import PartitionSpec as P

epsilon = 1e-06
loss_scale = 512.0
CHUNK = 64
WINDOW = 4
f32 = jnp.float32
bf16 = jnp.bfloat16


def column_tile(width, most):
    tile = most
    while width % tile:
        tile -= 128
    return tile


def split_columns(cols):
    unit = 256 if cols % 256 == 0 and cols >= 1024 else 128
    n = cols // unit
    last = max(1, (n + 3) // 6)
    first = (n - last + 1) // 2
    cuts = [0, first * unit, (n - last) * unit, cols]
    return list(zip(cuts[:-1], cuts[1:]))


def kernel(
    n_dp, n_mp, dt,
    th, tg_ref, tb_ref, sf, sg_ref, sb_ref, w,
    gp_out, gf_out, gain_out, bias_out, loss_out,
    wfull, gfull, normed, normed_t, own_hat, own_rs, target, proj, go, coef,
    stat_one, stat_two, pb, own_part, rx, zl, zr, zs, b_part, b_zl, b_zr, b_zs, b_x, gn_send, gn_recv,
    red_mp, red_x, red_z, red_a,
    ag_sems, gg_sems, nm_sems, s1_sems, s2_sems, gn_sems, rm_sems, rz_sems, rx_sems, rs_sems, rb_sems, bx_sems,
):
    length = n_dp // 2
    me = lax.axis_index("dp")
    m = lax.axis_index("mp")
    l = me // 2
    p = me % 2
    q = 1 - p
    x_dev = l * 2 + q
    right_dev = lax.rem(me + 2, n_dp)
    left_dev = lax.rem(me - 2 + n_dp, n_dp)
    tokens, cols = th.shape
    own, width = sf.shape
    rb = w.shape[0]
    chunks = split_columns(cols)
    tg, tb = tg_ref[...].reshape(1, cols), tb_ref[...].reshape(1, cols)
    sg, sb = sg_ref[...].reshape(1, width), sb_ref[...].reshape(1, width)

    def rows(j, n):
        return pl.ds(pl.multiple_of(j * n, n), n)

    def span(chunk):
        return pl.ds(chunk[0], chunk[1] - chunk[0])

    def remote(src, dst, ssem, rsem, device):
        return pltpu.make_async_remote_copy(
            src_ref=src, dst_ref=dst, send_sem=ssem, recv_sem=rsem,
            device_id=device, device_id_type=pl.DeviceIdType.MESH,
        )

    barrier = pltpu.get_barrier_semaphore()
    for k in range(1, n_mp):
        pl.semaphore_signal(barrier, inc=1, device_id={"mp": (m + k) % n_mp}, device_id_type=pl.DeviceIdType.MESH)
    for k in range(1, length):
        pl.semaphore_signal(
            barrier, inc=1, device_id={"dp": ((l + k) % length) * 2 + p}, device_id_type=pl.DeviceIdType.MESH
        )
    pl.semaphore_signal(barrier, inc=1, device_id={"dp": x_dev}, device_id_type=pl.DeviceIdType.MESH)
    pl.semaphore_wait(barrier, n_mp - 1 + length - 1 + 1)

    class Gather:
        def __init__(self, buf, sems, chunk, line_first):
            self.buf, self.sems, self.chunk, self.line_first = buf, sems, chunk, line_first
            self.lines = ((0, p),) if line_first else ((0, p), (1, q))

        def copy(self, lp, pp, ssem, rsem, device):
            ref = self.buf.at[rows(lp * 2 + pp, rb), span(self.chunk)]
            return remote(ref, ref, self.sems.at[ssem, lp], self.sems.at[rsem, lp], {"dp": device})

        def right(self, lp, pp, k):
            return self.copy(lp, pp, k, 2 + k, right_dev)

        def left(self, lp, pp, k):
            return self.copy(lp, pp, 4 + k, 2 + k, left_dev)

        def pair(self, lp, pp):
            return self.copy(lp, pp, 6, 7, x_dev)

        def forward_right(self, lp, pp, k):
            @pl.when(l + 1 < length)
            def _():
                self.right(lp, pp, k).start()

        def forward_left(self, lp, pp, k):
            @pl.when(l >= 1)
            def _():
                self.left(lp, pp, k).start()

        def begin(self):
            self.pair(l, p).start()
            self.forward_right(l, p, 0)
            self.forward_left(l, p, 0)

        def middle(self):
            self.pair(l, q).wait_recv()
            self.forward_right(l, q, 1)
            self.forward_left(l, q, 1)

        def step(self, s):
            a = l - s - 1
            b = l + s + 1
            for k, pp in self.lines:
                @pl.when(a >= 0)
                def _():
                    self.right(a, pp, k).wait_recv()
                    self.forward_right(a, pp, k)
                    if self.line_first:
                        self.pair(a, pp).start()

                @pl.when(b < length)
                def _():
                    self.left(b, pp, k).wait_recv()
                    self.forward_left(b, pp, k)
                    if self.line_first:
                        self.pair(b, pp).start()

        def finish(self):
            if self.line_first:
                @pl.loop(0, length)
                def _(lp):
                    self.pair(lp, q).wait_recv()

        def drain(self):
            @pl.loop(0, length)
            def _(lp):
                if self.line_first:
                    self.pair(lp, p).wait_send()
                for k, pp in self.lines:
                    @pl.when(jnp.logical_and(lp <= l, l + 1 < length))
                    def _():
                        self.right(lp, pp, k).wait_send()

                    @pl.when(jnp.logical_and(lp >= l, l >= 1))
                    def _():
                        self.left(lp, pp, k).wait_send()
            if not self.line_first:
                self.pair(l, p).wait_send()

    def gathers(buf, sems):
        return [Gather(buf, sems.at[i], chunks[i], i < 2) for i in range(3)]

    def mp_peers(make, act):
        for k in range(1, n_mp):
            act(make((m + k) % n_mp))

    def send_all(src, slots, sems):
        mp_peers(lambda d: remote(src(d), slots.at[m], sems.at[0, d], sems.at[1, m], {"mp": d}), lambda c: c.start())

    def recv_all(src, slots, sems):
        mp_peers(lambda d: remote(src(d), slots.at[d], sems.at[0, d], sems.at[1, d], {"mp": d}), lambda c: c.wait_recv())

    def drain_all(src, slots, sems):
        mp_peers(lambda d: remote(src(d), slots.at[m], sems.at[0, d], sems.at[1, m], {"mp": d}), lambda c: c.wait_send())

    gather_w = gathers(wfull, ag_sems)
    wfull[rows(me, rb)] = w[...]
    for g in (gather_w[2], gather_w[0], gather_w[1]):
        g.begin()

    lane = lax.broadcasted_iota(jnp.int32, (CHUNK, 128), 1)

    @pl.loop(0, tokens // CHUNK)
    def _(c):
        r = rows(c, CHUNK)
        v = th[r].astype(f32)
        mean = jnp.sum(v, axis=1, keepdims=True) / cols
        v = v - mean
        sq = jnp.sum(v * v, axis=1, keepdims=True)
        coef[r] = jnp.where(lane == 0, mean, jnp.where(lane == 1, sq, 0.0))

    stat_one[m] = coef[...].T[0:8]
    s1_src = lambda d: stat_one.at[m]
    send_all(s1_src, stat_one, s1_sems)
    for c in range(own // CHUNK):
        r = pl.ds(c * CHUNK, CHUNK)
        v = sf[r].astype(f32)
        v = v - jnp.mean(v, axis=1, keepdims=True)
        rs = lax.rsqrt(jnp.mean(v * v, axis=1, keepdims=True) + epsilon)
        hat = v * rs
        own_hat[r] = hat
        own_rs[r] = jnp.broadcast_to(rs, (CHUNK, 128))
        normed[m, r] = (hat * sg + sb).astype(bf16)
    nm_src = lambda d: normed.at[m]
    send_all(nm_src, normed, nm_sems)

    gather_w[2].middle()
    for g in gather_w:
        g.step(0)
    recv_all(s1_src, stat_one, s1_sems)
    mean = stat_one[0, 0:1]
    for k in range(1, n_mp):
        mean = mean + stat_one[k, 0:1]
    mean = mean / n_mp
    total = jnp.zeros_like(mean)
    for k in range(n_mp):
        gap = stat_one[k, 0:1] - mean
        total = total + (stat_one[k, 1:2] + cols * (gap * gap))
    scale = lax.rsqrt(total / dt + epsilon)
    coef[...] = jnp.concatenate([mean, scale, jnp.zeros((126, tokens), f32)], axis=0).T

    @pl.loop(0, tokens // CHUNK)
    def _(c):
        r = rows(c, CHUNK)
        cf = coef[r]
        t = (th[r].astype(f32) - cf[:, 0:1]) * cf[:, 1:2] * tg + tb
        target[r] = t
        coef[r] = jnp.where(lane == 2, jnp.sum(t * t, axis=1, keepdims=True), 0.0)

    recv_all(nm_src, normed, nm_sems)
    for k in range(n_mp):
        normed_t[:, pl.ds(k * own, own)] = normed[k].T

    @pl.loop(1, length - 1)
    def _(s):
        for g in gather_w:
            g.step(s)

    for g, (c0, c1) in zip(gather_w, chunks):
        g.finish()
        tile = column_tile(c1 - c0, 256)

        @pl.loop(0, (c1 - c0) // tile)
        def _(c):
            ct = pl.ds(pl.multiple_of(c0 + c * tile, 128), tile)
            proj[:, ct] = jnp.dot(
                normed[...].reshape(tokens, width), wfull[:, ct], preferred_element_type=f32
            )

        @pl.loop(0, tokens // CHUNK)
        def _(c):
            r = rows(c, CHUNK)
            pv, t = proj[r, c0:c1], target[r, c0:c1]
            inner = jnp.sum(pv * t, axis=1, keepdims=True)
            sq = jnp.sum(pv * pv, axis=1, keepdims=True)
            coef[r] = coef[r] + jnp.where(lane == 0, inner, jnp.where(lane == 1, sq, 0.0))

    stat_two[m] = coef[...].T[0:8]
    s2_src = lambda d: stat_two.at[m]
    send_all(s2_src, stat_two, s2_sems)
    recv_all(s2_src, stat_two, s2_sems)
    sums = stat_two[0]
    for k in range(1, n_mp):
        sums = sums + stat_two[k]
    inner = sums[0:1]
    norm_proj = jnp.sqrt(sums[1:2] + epsilon)
    norm_target = jnp.sqrt(sums[2:3] + epsilon)
    both = norm_proj * norm_target
    loss_part = jnp.sum(1.0 - inner / both, axis=1, keepdims=True)
    coef_proj = loss_scale * inner / (norm_proj * norm_proj * norm_proj * norm_target)
    coef_target = loss_scale / both
    coef[...] = jnp.concatenate([coef_proj, coef_target, jnp.zeros((126, tokens), f32)], axis=0).T

    def make_go(chunk):
        @pl.loop(0, tokens // CHUNK)
        def _(c):
            r = rows(c, CHUNK)
            cf = coef[r]
            ct = span(chunk)
            go[r, ct] = (cf[:, 0:1] * proj[r, ct] - cf[:, 1:2] * target[r, ct]).astype(bf16)

    near = jnp.minimum(l, length - 1 - l)
    alone = length - 1 - 2 * near

    def order(i):
        far = jnp.where(2 * l < length, length - 1 - i, i)
        k = jnp.maximum(i - alone, 0)
        d = near - k // 2
        return jnp.where(i < alone, far, jnp.where(k % 2 == 0, l + d, l - d))

    def partial(j, chunk):
        return jnp.dot(normed_t[rows(j, rb)], go[:, span(chunk)], preferred_element_type=f32)

    def x_copy(i, lp):
        part = span(chunks[i])
        return remote(pb.at[lp, :, part], rx.at[lp, :, part], rs_sems.at[i, 0, lp], rs_sems.at[i, 1, lp], {"dp": x_dev})

    def right_copy(i, lp):
        part = span(chunks[i])
        return remote(
            zs.at[lp, :, part], zl.at[lp, :, part], rs_sems.at[i, 2, lp], rs_sems.at[i, 3, lp], {"dp": right_dev}
        )

    def left_copy(i, lp):
        part = span(chunks[i])
        return remote(
            zs.at[lp, :, part], zr.at[lp, :, part], rs_sems.at[i, 4, lp], rs_sems.at[i, 5, lp], {"dp": left_dev}
        )

    def b_right(lp):
        return remote(b_zs.at[lp], b_zl.at[lp], rb_sems.at[0, lp], rb_sems.at[1, lp], {"dp": right_dev})

    def b_left(lp):
        return remote(b_zs.at[lp], b_zr.at[lp], rb_sems.at[2, lp], rb_sems.at[3, lp], {"dp": left_dev})

    def b_pair():
        return remote(b_zs.at[l, q], b_x, bx_sems.at[0], bx_sems.at[1], {"dp": x_dev})

    def scatter(i, n):
        lp = order(n)
        part = span(chunks[i])
        x_copy(i, lp).wait_recv()
        x_start(i * length + n + WINDOW)

        @pl.when(jnp.logical_and(lp >= l, l > 0))
        def _():
            right_copy(i, lp).wait_recv()
            own_part[lp, :, part] = own_part[lp, :, part] + zl[lp, :, part].astype(f32)

        @pl.when(jnp.logical_and(lp <= l, l < length - 1))
        def _():
            left_copy(i, lp).wait_recv()
            own_part[lp, :, part] = own_part[lp, :, part] + zr[lp, :, part].astype(f32)

        zs[lp, :, part] = (own_part[lp, :, part] + rx[lp, :, part].astype(f32)).astype(bf16)

        @pl.when(lp > l)
        def _():
            right_copy(i, lp).start()

        @pl.when(lp < l)
        def _():
            left_copy(i, lp).start()

    def b_scatter(lp):
        @pl.when(jnp.logical_and(lp >= l, l > 0))
        def _():
            b_right(lp).wait_recv()
            b_part[lp] = b_part[lp] + b_zl[lp].astype(f32)

        @pl.when(jnp.logical_and(lp <= l, l < length - 1))
        def _():
            b_left(lp).wait_recv()
            b_part[lp] = b_part[lp] + b_zr[lp].astype(f32)

        b_zs[lp] = b_part[lp].astype(bf16)

        @pl.when(lp > l)
        def _():
            b_right(lp).start()

        @pl.when(lp < l)
        def _():
            b_left(lp).start()

        @pl.when(lp == l)
        def _():
            b_pair().start()

    def x_start(k):
        @pl.when(k < length)
        def _():
            x_copy(0, order(k)).start()

        @pl.when(jnp.logical_and(k >= length, k < 2 * length))
        def _():
            x_copy(1, order(k - length)).start()

    def x_blocks(i):
        make_go(chunks[i])

        @pl.loop(0, length)
        def _(n):
            lp = order(n)
            pb[lp, :, span(chunks[i])] = partial(lp * 2 + q, chunks[i]).astype(bf16)
            if i == 0:
                @pl.when(n < WINDOW)
                def _():
                    x_start(n)

    x_blocks(0)
    last = chunks[2]
    make_go(last)
    b_part[...] = jnp.dot(normed_t[...], go[:, span(last)], preferred_element_type=f32).reshape(b_part.shape)
    at_end = jnp.logical_or(l == 0, l == length - 1)

    @pl.when(at_end)
    def _():
        @pl.loop(0, length - 1)
        def _(n):
            b_scatter(order(n))

    x_blocks(1)

    for i in range(2):
        @pl.loop(0, length)
        def _(n):
            lp = order(n)
            own_part[lp, :, span(chunks[i])] = partial(lp * 2 + p, chunks[i])

    band = 256

    @pl.loop(0, width // band)
    def _(c):
        ct = rows(c, band)
        g = lax.dot_general(go[...], wfull[ct], (((1,), (1,)), ((), ())), preferred_element_type=f32)
        for k in range(n_mp):
            gn_send[k, :, ct] = g[k * own:(k + 1) * own].astype(bf16)

    gn_src = lambda d: gn_send.at[d]
    send_all(gn_src, gn_recv, gn_sems)
    gn_recv[m] = gn_send[m]

    gather_g = gathers(gfull, gg_sems)

    @pl.loop(0, length)
    def _(n):
        lp = order(n)

        @pl.when(jnp.logical_or(jnp.logical_not(at_end), n == length - 1))
        def _():
            b_scatter(lp)

        scatter(0, n)

    gfull[rows(me, rb), span(chunks[0])] = zs[l, :, span(chunks[0])]
    gather_g[0].begin()

    scatter(1, 0)
    b_pair().wait_recv()
    gfull[rows(me, rb), span(last)] = (b_part[l, p] + b_x[...].astype(f32)).astype(bf16)
    gather_g[2].begin()

    recv_all(gn_src, gn_recv, gn_sems)
    gain_sum = jnp.zeros((1, width), f32)
    bias_sum = jnp.zeros((1, width), f32)
    for c in range(own // CHUNK):
        r = pl.ds(c * CHUNK, CHUNK)
        g = gn_recv[0, r].astype(f32)
        for k in range(1, n_mp):
            g = g + gn_recv[k, r].astype(f32)
        hat = own_hat[r]
        gain_sum = gain_sum + jnp.sum(g * hat, axis=0, keepdims=True)
        bias_sum = bias_sum + jnp.sum(g, axis=0, keepdims=True)
        g = g * sg
        g = g - jnp.mean(g, axis=1, keepdims=True) - hat * jnp.mean(g * hat, axis=1, keepdims=True)
        gf_out[r] = (own_rs[r][:, 0:1] * g).astype(bf16)
    red_mp[m] = jnp.concatenate(
        [gain_sum, bias_sum, jnp.broadcast_to(loss_part, (1, width)), jnp.zeros((5, width), f32)], axis=0
    )
    rm_src = lambda d: red_mp.at[m]
    send_all(rm_src, red_mp, rm_sems)
    gather_g[0].step(0)
    gather_g[2].middle()

    @pl.loop(1, length - 1)
    def _(n):
        scatter(1, n)
        gather_g[0].step(n)
        gather_g[2].step(n - 1)

    scatter(1, length - 1)
    gfull[rows(me, rb), span(chunks[1])] = zs[l, :, span(chunks[1])]
    gather_g[1].begin()
    gather_g[2].step(length - 2)

    recv_all(rm_src, red_mp, rm_sems)
    acc = red_mp[0]
    for k in range(1, n_mp):
        acc = acc + red_mp[k]
    red_a[...] = acc
    pair = remote(red_a, red_x, rx_sems.at[0], rx_sems.at[1], {"dp": x_dev})
    pair.start()
    gather_g[1].step(0)
    pair.wait_recv()
    red_z[l] = red_a[...] + red_x[...]

    def line_copy(d, slot):
        return remote(red_z.at[l], red_z.at[slot], rz_sems.at[0, d], rz_sems.at[1, slot], {"dp": d * 2 + p})

    for k in range(1, length):
        line_copy((l + k) % length, l).start()

    @pl.loop(1, length - 1)
    def _(s):
        gather_g[1].step(s)

    for k in range(1, length):
        line_copy((l + k) % length, (l + k) % length).wait_recv()
    acc = red_z[0]
    for k in range(1, length):
        acc = acc + red_z[k]
    gain_out[...] = acc[0:1].reshape(width)
    bias_out[...] = acc[1:2].reshape(width)
    loss_out[...] = acc[2:3, 0:128] / (n_mp * tokens * n_dp)

    gather_g[0].finish()
    gather_g[2].finish()
    gather_g[1].finish()
    gp_out[...] = gfull[...]

    for g in gather_w + gather_g:
        g.drain()
    drain_all(nm_src, normed, nm_sems)
    drain_all(s1_src, stat_one, s1_sems)
    drain_all(s2_src, stat_two, s2_sems)
    drain_all(gn_src, gn_recv, gn_sems)
    drain_all(rm_src, red_mp, rm_sems)
    pair.wait_send()
    for k in range(1, length):
        line_copy((l + k) % length, l).wait_send()
    b_pair().wait_send()

    @pl.loop(0, length)
    def _(lp):
        for i in range(2):
            x_copy(i, lp).wait_send()

        @pl.when(lp > l)
        def _():
            for i in range(2):
                right_copy(i, lp).wait_send()
            b_right(lp).wait_send()

        @pl.when(lp < l)
        def _():
            for i in range(2):
                left_copy(i, lp).wait_send()
            b_left(lp).wait_send()


def per_device(n_dp, n_mp, dt, th, tg, tb, sf, sg, sb, w):
    tokens, cols = th.shape
    own, width = sf.shape
    rb = w.shape[0]
    length = n_dp // 2
    chunks = split_columns(cols)
    bw = chunks[2][1] - chunks[2][0]
    vmem = pltpu.VMEM
    dma = pltpu.SemaphoreType.DMA
    scratch = [
        vmem((width, cols), bf16),
        vmem((width, cols), bf16),
        vmem((n_mp, own, width), bf16),
        vmem((width, tokens), bf16),
        vmem((own, width), f32),
        vmem((own, 128), f32),
        vmem((tokens, cols), f32),
        vmem((tokens, cols), f32),
        vmem((tokens, cols), bf16),
        vmem((tokens, 128), f32),
        vmem((n_mp, 8, tokens), f32),
        vmem((n_mp, 8, tokens), f32),
        vmem((length, rb, cols), bf16),
        vmem((length, rb, cols), f32),
        vmem((length, rb, cols), bf16),
        vmem((length, rb, cols), bf16),
        vmem((length, rb, cols), bf16),
        vmem((length, rb, cols), bf16),
        vmem((length, 2, rb, bw), f32),
        vmem((length, 2, rb, bw), bf16),
        vmem((length, 2, rb, bw), bf16),
        vmem((length, 2, rb, bw), bf16),
        vmem((rb, bw), bf16),
        vmem((n_mp, own, width), bf16),
        vmem((n_mp, own, width), bf16),
        vmem((n_mp, 8, width), f32),
        vmem((8, width), f32),
        vmem((length, 8, width), f32),
        vmem((8, width), f32),
        dma((3, 8, length)), dma((3, 8, length)),
        dma((2, n_mp)), dma((2, n_mp)), dma((2, n_mp)), dma((2, n_mp)), dma((2, n_mp)),
        dma((2, length)), dma((2,)), dma((2, 6, length)), dma((4, length)), dma((2,)),
    ]
    whole = pl.BlockSpec(memory_space=pltpu.VMEM)
    grad_proj, grad_feats, gain, bias, loss = pl.pallas_call(
        functools.partial(kernel, n_dp, n_mp, dt),
        out_shape=(
            jax.ShapeDtypeStruct((width, cols), bf16),
            jax.ShapeDtypeStruct((own, width), bf16),
            jax.ShapeDtypeStruct((width,), f32),
            jax.ShapeDtypeStruct((width,), f32),
            jax.ShapeDtypeStruct((1, 128), f32),
        ),
        in_specs=[whole] * 7,
        out_specs=(whole,) * 5,
        scratch_shapes=scratch,
        compiler_params=pltpu.CompilerParams(
            collective_id=0, has_side_effects=True, vmem_limit_bytes=56 * 1024 * 1024
        ),
    )(th, tg, tb, sf, sg, sb, w)
    return (loss[0, 0], grad_proj.astype(f32), grad_feats, gain, bias)


def solution(mesh):
    n_dp, n_mp = mesh.shape["dp"], mesh.shape["mp"]

    def run(th, tg, tb, sf, sg, sb, w):
        in_specs = (P("dp", "mp"), P("mp"), P("mp"), P(("dp", "mp"), None), P(), P(), P("dp", "mp"))
        out_specs = (P(), P(None, "mp"), P(("dp", "mp"), None), P(), P())
        return jax.shard_map(
            functools.partial(per_device, n_dp, n_mp, th.shape[1]),
            mesh=mesh, in_specs=in_specs, out_specs=out_specs, check_vma=False,
        )(th, tg, tb, sf, sg, sb, w)

    return run
```

```python
import functools

import jax
import jax.numpy as jnp
from jax import lax
from jax.experimental import pallas as pl
from jax.experimental.pallas import tpu as pltpu
from jax.sharding import PartitionSpec as P

epsilon = 1e-06
loss_scale = 512.0
CHUNK = 128
WINDOW = 4
f32 = jnp.float32
bf16 = jnp.bfloat16


def column_tile(width, most):
    tile = most
    while width % tile:
        tile -= 128
    return tile


def split_columns(cols):
    unit = 256 if cols % 256 == 0 and cols >= 1024 else 128
    n = cols // unit
    last = max(1, (n + 3) // 6)
    first = (n - last + 1) // 2
    cuts = [0, first * unit, (n - last) * unit, cols]
    return list(zip(cuts[:-1], cuts[1:]))


def kernel(
    n_dp, n_mp, dt,
    th_hbm, tg_ref, tb_ref, sf_hbm, sg_ref, sb_ref, w,
    gp_out, gf_out, gain_out, bias_out, loss_out,
    wfull, gfull, normed, normed_t, own_hat, own_rs, target, proj, go, coef,
    stat_one, stat_two, pb, own_part, rx, zl, zr, zs, b_part, b_zl, b_zr, b_zs, b_x, gn_send, gn_recv,
    red_mp, red_x, red_z, red_a, th, sf, in_sems, out_sems,
    ag_sems, gg_sems, nm_sems, s1_sems, s2_sems, gn_sems, rm_sems, rz_sems, rx_sems, rs_sems, rb_sems, bx_sems,
):
    load_th = pltpu.make_async_copy(th_hbm, th, in_sems.at[0])
    load_sf = pltpu.make_async_copy(sf_hbm, sf, in_sems.at[1])
    load_th.start()
    load_sf.start()
    length = n_dp // 2
    me = lax.axis_index("dp")
    m = lax.axis_index("mp")
    l = me // 2
    p = me % 2
    q = 1 - p
    x_dev = l * 2 + q
    right_dev = lax.rem(me + 2, n_dp)
    left_dev = lax.rem(me - 2 + n_dp, n_dp)
    tokens, cols = th.shape
    own, width = sf.shape
    rb = w.shape[0]
    chunks = split_columns(cols)
    tg, tb = tg_ref[...].reshape(1, cols), tb_ref[...].reshape(1, cols)
    sg, sb = sg_ref[...].reshape(1, width), sb_ref[...].reshape(1, width)

    def rows(j, n):
        return pl.ds(pl.multiple_of(j * n, n), n)

    def span(chunk):
        return pl.ds(chunk[0], chunk[1] - chunk[0])

    def remote(src, dst, ssem, rsem, device):
        return pltpu.make_async_remote_copy(
            src_ref=src, dst_ref=dst, send_sem=ssem, recv_sem=rsem,
            device_id=device, device_id_type=pl.DeviceIdType.MESH,
        )

    barrier = pltpu.get_barrier_semaphore()
    for k in range(1, n_mp):
        pl.semaphore_signal(barrier, inc=1, device_id={"mp": (m + k) % n_mp}, device_id_type=pl.DeviceIdType.MESH)
    for k in range(1, length):
        pl.semaphore_signal(
            barrier, inc=1, device_id={"dp": ((l + k) % length) * 2 + p}, device_id_type=pl.DeviceIdType.MESH
        )
    pl.semaphore_signal(barrier, inc=1, device_id={"dp": x_dev}, device_id_type=pl.DeviceIdType.MESH)
    pl.semaphore_wait(barrier, n_mp - 1 + length - 1 + 1)

    class Gather:
        def __init__(self, buf, sems, chunk, line_first):
            self.buf, self.sems, self.chunk, self.line_first = buf, sems, chunk, line_first
            self.lines = ((0, p),) if line_first else ((0, p), (1, q))

        def copy(self, lp, pp, ssem, rsem, device):
            ref = self.buf.at[rows(lp * 2 + pp, rb), span(self.chunk)]
            return remote(ref, ref, self.sems.at[ssem, lp], self.sems.at[rsem, lp], {"dp": device})

        def right(self, lp, pp, k):
            return self.copy(lp, pp, k, 2 + k, right_dev)

        def left(self, lp, pp, k):
            return self.copy(lp, pp, 4 + k, 2 + k, left_dev)

        def pair(self, lp, pp):
            return self.copy(lp, pp, 6, 7, x_dev)

        def forward_right(self, lp, pp, k):
            @pl.when(l + 1 < length)
            def _():
                self.right(lp, pp, k).start()

        def forward_left(self, lp, pp, k):
            @pl.when(l >= 1)
            def _():
                self.left(lp, pp, k).start()

        def begin(self):
            self.pair(l, p).start()
            self.forward_right(l, p, 0)
            self.forward_left(l, p, 0)

        def middle(self):
            self.pair(l, q).wait_recv()
            self.forward_right(l, q, 1)
            self.forward_left(l, q, 1)

        def step(self, s):
            a = l - s - 1
            b = l + s + 1
            for k, pp in self.lines:
                @pl.when(a >= 0)
                def _():
                    self.right(a, pp, k).wait_recv()
                    self.forward_right(a, pp, k)
                    if self.line_first:
                        self.pair(a, pp).start()

                @pl.when(b < length)
                def _():
                    self.left(b, pp, k).wait_recv()
                    self.forward_left(b, pp, k)
                    if self.line_first:
                        self.pair(b, pp).start()

        def finish(self):
            if self.line_first:
                @pl.loop(0, length)
                def _(lp):
                    self.pair(lp, q).wait_recv()

        def drain(self):
            @pl.loop(0, length)
            def _(lp):
                if self.line_first:
                    self.pair(lp, p).wait_send()
                for k, pp in self.lines:
                    @pl.when(jnp.logical_and(lp <= l, l + 1 < length))
                    def _():
                        self.right(lp, pp, k).wait_send()

                    @pl.when(jnp.logical_and(lp >= l, l >= 1))
                    def _():
                        self.left(lp, pp, k).wait_send()
            if not self.line_first:
                self.pair(l, p).wait_send()

    def gathers(buf, sems):
        return [Gather(buf, sems.at[i], chunks[i], i < 2) for i in range(3)]

    def mp_peers(make, act):
        for k in range(1, n_mp):
            act(make((m + k) % n_mp))

    def send_all(src, slots, sems):
        mp_peers(lambda d: remote(src(d), slots.at[m], sems.at[0, d], sems.at[1, m], {"mp": d}), lambda c: c.start())

    def recv_all(src, slots, sems):
        mp_peers(lambda d: remote(src(d), slots.at[d], sems.at[0, d], sems.at[1, d], {"mp": d}), lambda c: c.wait_recv())

    def drain_all(src, slots, sems):
        mp_peers(lambda d: remote(src(d), slots.at[m], sems.at[0, d], sems.at[1, m], {"mp": d}), lambda c: c.wait_send())

    gather_w = gathers(wfull, ag_sems)
    wfull[rows(me, rb)] = w[...]
    for g in (gather_w[2], gather_w[0], gather_w[1]):
        g.begin()

    lane = lax.broadcasted_iota(jnp.int32, (CHUNK, 128), 1)

    load_th.wait()
    load_sf.wait()

    @pl.loop(0, tokens // CHUNK)
    def _(c):
        r = rows(c, CHUNK)
        v = th[r].astype(f32)
        mean = jnp.sum(v, axis=1, keepdims=True) / cols
        v = v - mean
        sq = jnp.sum(v * v, axis=1, keepdims=True)
        coef[r] = jnp.where(lane == 0, mean, jnp.where(lane == 1, sq, 0.0))

    stat_one[m] = coef[...].T[0:8]
    s1_src = lambda d: stat_one.at[m]
    send_all(s1_src, stat_one, s1_sems)
    for c in range(own // CHUNK):
        r = pl.ds(c * CHUNK, CHUNK)
        v = sf[r].astype(f32)
        v = v - jnp.mean(v, axis=1, keepdims=True)
        rs = lax.rsqrt(jnp.mean(v * v, axis=1, keepdims=True) + epsilon)
        hat = v * rs
        own_hat[r] = hat
        own_rs[r] = jnp.broadcast_to(rs, (CHUNK, 128))
        normed[m, r] = (hat * sg + sb).astype(bf16)
    nm_src = lambda d: normed.at[m]
    send_all(nm_src, normed, nm_sems)

    gather_w[2].middle()
    for g in gather_w:
        g.step(0)
    recv_all(s1_src, stat_one, s1_sems)
    mean = stat_one[0, 0:1]
    for k in range(1, n_mp):
        mean = mean + stat_one[k, 0:1]
    mean = mean / n_mp
    total = jnp.zeros_like(mean)
    for k in range(n_mp):
        gap = stat_one[k, 0:1] - mean
        total = total + (stat_one[k, 1:2] + cols * (gap * gap))
    scale = lax.rsqrt(total / dt + epsilon)
    coef[...] = jnp.concatenate([mean, scale, jnp.zeros((126, tokens), f32)], axis=0).T

    @pl.loop(0, tokens // CHUNK)
    def _(c):
        r = rows(c, CHUNK)
        cf = coef[r]
        t = (th[r].astype(f32) - cf[:, 0:1]) * cf[:, 1:2] * tg + tb
        target[r] = t
        coef[r] = jnp.where(lane == 2, jnp.sum(t * t, axis=1, keepdims=True), 0.0)

    recv_all(nm_src, normed, nm_sems)
    for k in range(n_mp):
        normed_t[:, pl.ds(k * own, own)] = normed[k].T

    @pl.loop(1, length - 1)
    def _(s):
        for g in gather_w:
            g.step(s)

    for g, (c0, c1) in zip(gather_w, chunks):
        g.finish()
        tile = column_tile(c1 - c0, 256)

        @pl.loop(0, (c1 - c0) // tile)
        def _(c):
            ct = pl.ds(pl.multiple_of(c0 + c * tile, 128), tile)
            proj[:, ct] = jnp.dot(
                normed[...].reshape(tokens, width), wfull[:, ct], preferred_element_type=f32
            )

        @pl.loop(0, tokens // CHUNK)
        def _(c):
            r = rows(c, CHUNK)
            pv, t = proj[r, c0:c1], target[r, c0:c1]
            inner = jnp.sum(pv * t, axis=1, keepdims=True)
            sq = jnp.sum(pv * pv, axis=1, keepdims=True)
            coef[r] = coef[r] + jnp.where(lane == 0, inner, jnp.where(lane == 1, sq, 0.0))

    stat_two[m] = coef[...].T[0:8]
    s2_src = lambda d: stat_two.at[m]
    send_all(s2_src, stat_two, s2_sems)
    recv_all(s2_src, stat_two, s2_sems)
    sums = stat_two[0]
    for k in range(1, n_mp):
        sums = sums + stat_two[k]
    inner = sums[0:1]
    norm_proj = jnp.sqrt(sums[1:2] + epsilon)
    norm_target = jnp.sqrt(sums[2:3] + epsilon)
    both = norm_proj * norm_target
    loss_part = jnp.sum(1.0 - inner / both, axis=1, keepdims=True)
    coef_proj = loss_scale * inner / (norm_proj * norm_proj * norm_proj * norm_target)
    coef_target = loss_scale / both
    coef[...] = jnp.concatenate([coef_proj, coef_target, jnp.zeros((126, tokens), f32)], axis=0).T

    def make_go(chunk):
        @pl.loop(0, tokens // CHUNK)
        def _(c):
            r = rows(c, CHUNK)
            cf = coef[r]
            ct = span(chunk)
            go[r, ct] = (cf[:, 0:1] * proj[r, ct] - cf[:, 1:2] * target[r, ct]).astype(bf16)

    near = jnp.minimum(l, length - 1 - l)
    alone = length - 1 - 2 * near

    def order(i):
        far = jnp.where(2 * l < length, length - 1 - i, i)
        k = jnp.maximum(i - alone, 0)
        d = near - k // 2
        return jnp.where(i < alone, far, jnp.where(k % 2 == 0, l + d, l - d))

    def partial(j, chunk):
        return jnp.dot(normed_t[rows(j, rb)], go[:, span(chunk)], preferred_element_type=f32)

    def x_copy(i, lp):
        part = span(chunks[i])
        return remote(pb.at[lp, :, part], rx.at[lp, :, part], rs_sems.at[i, 0, lp], rs_sems.at[i, 1, lp], {"dp": x_dev})

    def right_copy(i, lp):
        part = span(chunks[i])
        return remote(
            zs.at[lp, :, part], zl.at[lp, :, part], rs_sems.at[i, 2, lp], rs_sems.at[i, 3, lp], {"dp": right_dev}
        )

    def left_copy(i, lp):
        part = span(chunks[i])
        return remote(
            zs.at[lp, :, part], zr.at[lp, :, part], rs_sems.at[i, 4, lp], rs_sems.at[i, 5, lp], {"dp": left_dev}
        )

    def b_right(lp):
        return remote(b_zs.at[lp], b_zl.at[lp], rb_sems.at[0, lp], rb_sems.at[1, lp], {"dp": right_dev})

    def b_left(lp):
        return remote(b_zs.at[lp], b_zr.at[lp], rb_sems.at[2, lp], rb_sems.at[3, lp], {"dp": left_dev})

    def b_pair():
        return remote(b_zs.at[l, q], b_x, bx_sems.at[0], bx_sems.at[1], {"dp": x_dev})

    def scatter(i, n):
        lp = order(n)
        part = span(chunks[i])
        x_copy(i, lp).wait_recv()
        x_start(i * length + n + WINDOW)

        @pl.when(jnp.logical_and(lp >= l, l > 0))
        def _():
            right_copy(i, lp).wait_recv()
            own_part[lp, :, part] = own_part[lp, :, part] + zl[lp, :, part].astype(f32)

        @pl.when(jnp.logical_and(lp <= l, l < length - 1))
        def _():
            left_copy(i, lp).wait_recv()
            own_part[lp, :, part] = own_part[lp, :, part] + zr[lp, :, part].astype(f32)

        zs[lp, :, part] = (own_part[lp, :, part] + rx[lp, :, part].astype(f32)).astype(bf16)

        @pl.when(lp > l)
        def _():
            right_copy(i, lp).start()

        @pl.when(lp < l)
        def _():
            left_copy(i, lp).start()

    def b_scatter(lp):
        @pl.when(jnp.logical_and(lp >= l, l > 0))
        def _():
            b_right(lp).wait_recv()
            b_part[lp] = b_part[lp] + b_zl[lp].astype(f32)

        @pl.when(jnp.logical_and(lp <= l, l < length - 1))
        def _():
            b_left(lp).wait_recv()
            b_part[lp] = b_part[lp] + b_zr[lp].astype(f32)

        b_zs[lp] = b_part[lp].astype(bf16)

        @pl.when(lp > l)
        def _():
            b_right(lp).start()

        @pl.when(lp < l)
        def _():
            b_left(lp).start()

        @pl.when(lp == l)
        def _():
            b_pair().start()

    def x_start(k):
        @pl.when(k < length)
        def _():
            x_copy(0, order(k)).start()

        @pl.when(jnp.logical_and(k >= length, k < 2 * length))
        def _():
            x_copy(1, order(k - length)).start()

    def x_blocks(i):
        make_go(chunks[i])

        @pl.loop(0, length)
        def _(n):
            lp = order(n)
            pb[lp, :, span(chunks[i])] = partial(lp * 2 + q, chunks[i]).astype(bf16)
            if i == 0:
                @pl.when(n < WINDOW)
                def _():
                    x_start(n)

    x_blocks(0)
    last = chunks[2]
    make_go(last)
    b_part[...] = jnp.dot(normed_t[...], go[:, span(last)], preferred_element_type=f32).reshape(b_part.shape)
    at_end = jnp.logical_or(l == 0, l == length - 1)

    @pl.when(at_end)
    def _():
        @pl.loop(0, length - 1)
        def _(n):
            b_scatter(order(n))

    make_go(chunks[1])

    def own_block(i, n):
        lp = order(n)
        own_part[lp, :, span(chunks[i])] = partial(lp * 2 + p, chunks[i])

    @pl.loop(0, length)
    def _(n):
        own_block(0, n)

    band = 256

    @pl.loop(0, width // band)
    def _(c):
        ct = rows(c, band)
        g = lax.dot_general(go[...], wfull[ct], (((1,), (1,)), ((), ())), preferred_element_type=f32)
        for k in range(n_mp):
            gn_send[k, :, ct] = g[k * own:(k + 1) * own].astype(bf16)

    gn_src = lambda d: gn_send.at[d]
    send_all(gn_src, gn_recv, gn_sems)
    gn_recv[m] = gn_send[m]

    gather_g = gathers(gfull, gg_sems)

    @pl.loop(0, length)
    def _(n):
        lp = order(n)

        @pl.when(jnp.logical_or(jnp.logical_not(at_end), n == length - 1))
        def _():
            b_scatter(lp)

        pb[order(n), :, span(chunks[1])] = partial(order(n) * 2 + q, chunks[1]).astype(bf16)
        scatter(0, n)
        own_block(1, n)

    gfull[rows(me, rb), span(chunks[0])] = zs[l, :, span(chunks[0])]
    gather_g[0].begin()

    scatter(1, 0)
    b_pair().wait_recv()
    gfull[rows(me, rb), span(last)] = (b_part[l, p] + b_x[...].astype(f32)).astype(bf16)
    gather_g[2].begin()

    recv_all(gn_src, gn_recv, gn_sems)
    gain_sum = jnp.zeros((1, width), f32)
    bias_sum = jnp.zeros((1, width), f32)
    for c in range(own // CHUNK):
        r = pl.ds(c * CHUNK, CHUNK)
        g = gn_recv[0, r].astype(f32)
        for k in range(1, n_mp):
            g = g + gn_recv[k, r].astype(f32)
        hat = own_hat[r]
        gain_sum = gain_sum + jnp.sum(g * hat, axis=0, keepdims=True)
        bias_sum = bias_sum + jnp.sum(g, axis=0, keepdims=True)
        g = g * sg
        g = g - jnp.mean(g, axis=1, keepdims=True) - hat * jnp.mean(g * hat, axis=1, keepdims=True)
        gf_out[r] = (own_rs[r][:, 0:1] * g).astype(bf16)
    red_mp[m] = jnp.concatenate(
        [gain_sum, bias_sum, jnp.broadcast_to(loss_part, (1, width)), jnp.zeros((5, width), f32)], axis=0
    )
    rm_src = lambda d: red_mp.at[m]
    send_all(rm_src, red_mp, rm_sems)
    gather_g[0].step(0)
    gather_g[2].middle()

    @pl.loop(1, length - 1)
    def _(n):
        scatter(1, n)
        gather_g[0].step(n)
        gather_g[2].step(n - 1)

    scatter(1, length - 1)
    gfull[rows(me, rb), span(chunks[1])] = zs[l, :, span(chunks[1])]
    gather_g[1].begin()
    gather_g[2].step(length - 2)

    recv_all(rm_src, red_mp, rm_sems)
    acc = red_mp[0]
    for k in range(1, n_mp):
        acc = acc + red_mp[k]
    red_a[...] = acc
    pair = remote(red_a, red_x, rx_sems.at[0], rx_sems.at[1], {"dp": x_dev})
    pair.start()
    gather_g[1].step(0)
    pair.wait_recv()
    red_z[l] = red_a[...] + red_x[...]

    def line_copy(d, slot):
        return remote(red_z.at[l], red_z.at[slot], rz_sems.at[0, d], rz_sems.at[1, slot], {"dp": d * 2 + p})

    for k in range(1, length):
        line_copy((l + k) % length, l).start()

    @pl.loop(1, length - 1)
    def _(s):
        gather_g[1].step(s)

    for k in range(1, length):
        line_copy((l + k) % length, (l + k) % length).wait_recv()
    acc = red_z[0]
    for k in range(1, length):
        acc = acc + red_z[k]
    gain_out[...] = acc[0:1].reshape(width)
    bias_out[...] = acc[1:2].reshape(width)
    loss_out[...] = acc[2:3, 0:128] / (n_mp * tokens * n_dp)

    def out_copy(i):
        part = span(chunks[i])
        return pltpu.make_async_copy(gfull.at[:, part], gp_out.at[:, part], out_sems.at[i])

    for i in (0, 2, 1):
        gather_g[i].finish()
        out_copy(i).start()

    for g in gather_w + gather_g:
        g.drain()
    drain_all(nm_src, normed, nm_sems)
    drain_all(s1_src, stat_one, s1_sems)
    drain_all(s2_src, stat_two, s2_sems)
    drain_all(gn_src, gn_recv, gn_sems)
    drain_all(rm_src, red_mp, rm_sems)
    pair.wait_send()
    for k in range(1, length):
        line_copy((l + k) % length, l).wait_send()
    b_pair().wait_send()
    for i in range(3):
        out_copy(i).wait()

    @pl.loop(0, length)
    def _(lp):
        for i in range(2):
            x_copy(i, lp).wait_send()

        @pl.when(lp > l)
        def _():
            for i in range(2):
                right_copy(i, lp).wait_send()
            b_right(lp).wait_send()

        @pl.when(lp < l)
        def _():
            for i in range(2):
                left_copy(i, lp).wait_send()
            b_left(lp).wait_send()


def per_device(n_dp, n_mp, dt, th, tg, tb, sf, sg, sb, w):
    tokens, cols = th.shape
    own, width = sf.shape
    rb = w.shape[0]
    length = n_dp // 2
    chunks = split_columns(cols)
    bw = chunks[2][1] - chunks[2][0]
    vmem = pltpu.VMEM
    dma = pltpu.SemaphoreType.DMA
    scratch = [
        vmem((width, cols), bf16),
        vmem((width, cols), bf16),
        vmem((n_mp, own, width), bf16),
        vmem((width, tokens), bf16),
        vmem((own, width), f32),
        vmem((own, 128), f32),
        vmem((tokens, cols), f32),
        vmem((tokens, cols), f32),
        vmem((tokens, cols), bf16),
        vmem((tokens, 128), f32),
        vmem((n_mp, 8, tokens), f32),
        vmem((n_mp, 8, tokens), f32),
        vmem((length, rb, cols), bf16),
        vmem((length, rb, cols), f32),
        vmem((length, rb, cols), bf16),
        vmem((length, rb, cols), bf16),
        vmem((length, rb, cols), bf16),
        vmem((length, rb, cols), bf16),
        vmem((length, 2, rb, bw), f32),
        vmem((length, 2, rb, bw), bf16),
        vmem((length, 2, rb, bw), bf16),
        vmem((length, 2, rb, bw), bf16),
        vmem((rb, bw), bf16),
        vmem((n_mp, own, width), bf16),
        vmem((n_mp, own, width), bf16),
        vmem((n_mp, 8, width), f32),
        vmem((8, width), f32),
        vmem((length, 8, width), f32),
        vmem((8, width), f32),
        vmem((tokens, cols), bf16),
        vmem((own, width), bf16),
        dma((2,)),
        dma((3,)),
        dma((3, 8, length)), dma((3, 8, length)),
        dma((2, n_mp)), dma((2, n_mp)), dma((2, n_mp)), dma((2, n_mp)), dma((2, n_mp)),
        dma((2, length)), dma((2,)), dma((2, 6, length)), dma((4, length)), dma((2,)),
    ]
    whole = pl.BlockSpec(memory_space=pltpu.VMEM)
    hbm = pl.BlockSpec(memory_space=pl.ANY)
    grad_proj, grad_feats, gain, bias, loss = pl.pallas_call(
        functools.partial(kernel, n_dp, n_mp, dt),
        out_shape=(
            jax.ShapeDtypeStruct((width, cols), bf16),
            jax.ShapeDtypeStruct((own, width), bf16),
            jax.ShapeDtypeStruct((width,), f32),
            jax.ShapeDtypeStruct((width,), f32),
            jax.ShapeDtypeStruct((1, 128), f32),
        ),
        in_specs=[hbm, whole, whole, hbm, whole, whole, whole],
        out_specs=(hbm,) + (whole,) * 4,
        scratch_shapes=scratch,
        compiler_params=pltpu.CompilerParams(
            collective_id=0, has_side_effects=True, vmem_limit_bytes=56 * 1024 * 1024
        ),
    )(th, tg, tb, sf, sg, sb, w)
    return (loss[0, 0], grad_proj.astype(f32), grad_feats, gain, bias)


def solution(mesh):
    n_dp, n_mp = mesh.shape["dp"], mesh.shape["mp"]

    def run(th, tg, tb, sf, sg, sb, w):
        in_specs = (P("dp", "mp"), P("mp"), P("mp"), P(("dp", "mp"), None), P(), P(), P("dp", "mp"))
        out_specs = (P(), P(None, "mp"), P(("dp", "mp"), None), P(), P())
        return jax.shard_map(
            functools.partial(per_device, n_dp, n_mp, th.shape[1]),
            mesh=mesh, in_specs=in_specs, out_specs=out_specs, check_vma=False,
        )(th, tg, tb, sf, sg, sb, w)

    return run
```
